32 devices in a mesh: pipe: 4 (over x, core), dp: 2 (over y), vocab: 4 (over z).
Axes of the slice: x: 2, y: 2, z: 4, core: 2. Of those that a mesh axis runs over, the one named last changes fastest.
Arguments:
- hidden: bfloat16 [512, 4608], P(('pipe', 'dp', 'vocab')), may hold values from -6 to 6
- targets: int32 [512], P(('pipe', 'dp', 'vocab')), may hold values from 0 to 12287, as said below
- input_ids: int32 [512], P(('pipe', 'dp', 'vocab')), may hold values from 0 to 12287, as said below
- input_grads: bfloat16 [512, 4608], P(('pipe', 'dp', 'vocab')), may hold values from -0.3125 to 0.3125
- table: bfloat16 [12288, 4608], P(('pipe', 'vocab'), 'dp'), may hold values from -0.75 to 0.75
- keep: int32 [12288], P(('pipe', 'vocab')), may hold values from 0 to 1
- first_moment: bfloat16 [12288, 4608], P(('pipe', 'vocab'), 'dp'), may hold values from -0.015625 to 0.015625
- second_moment: bfloat16 [12288, 4608], P(('pipe', 'vocab'), 'dp'), may hold values from 9.983778e-07 to 9.953976e-06
Outputs:
- new_table: bfloat16 [12288, 4608], P(('pipe', 'vocab'), 'dp')
- new_first: bfloat16 [12288, 4608], P(('pipe', 'vocab'), 'dp')
- new_second: bfloat16 [12288, 4608], P(('pipe', 'vocab'), 'dp')
- loss: float32 [], replicated
The draws below stay inside these ranges and needn't reach their ends.
Inputs may be any that keep to these rules, and one draw needn't show every extreme that they name: `targets`: names only rows with keep = 1. `input_ids`: names only rows with keep = 1.
All inputs are finite; a program needn't handle non-finite values.
Results may differ from the reference program's by a relative error of at most 0.0036.
Values may be sent and summed in bfloat16 or wider, within the bound.
A program may use at most 192 MiB of HBM per device.

```python
import math
import jax
import jax.numpy as jnp
from jax import lax

D = 4608
VR = 768
TOKENS = 512
VOCAB = 12288


def keep_rows(key):
    groups = VOCAB // VR
    thresholds = jax.random.randint(jax.random.fold_in(key, 7), (groups,), 0, 400)
    values = jax.random.randint(jax.random.fold_in(key, 8), (VOCAB,), 0, 1000)
    return (values >= jnp.repeat(thresholds, VR)).astype(jnp.int32)


def pick_kept(key, keep, count):
    running = jnp.cumsum(keep)
    total = running[-1]
    picks = jax.random.randint(key, (count,), 0, total)
    return jnp.searchsorted(running, picks, side='right').astype(jnp.int32)


def draw_keep(key, part):
    return keep_rows(key)


def draw_targets(key, part):
    return pick_kept(jax.random.fold_in(key, 11), keep_rows(key), TOKENS)


def draw_input_ids(key, part):
    return pick_kept(jax.random.fold_in(key, 13), keep_rows(key), TOKENS)


def block_scale(rng, dims, split, smallest, top_value):
    level, own = 1.0, jax.random.fold_in(rng, 6)
    for dim, blocks in split:
        heights = jnp.exp(jax.random.uniform(jax.random.fold_in(own, dim), (blocks,), jnp.float32, smallest / len(split), top_value / len(split)))
        level = level * jnp.repeat(heights, dims[dim] // blocks).reshape([-1 if axis == dim else 1 for axis in range(len(dims))])
    return level


def gaussian(stream_key, dims, deviation, most, cuts=(), kind=jnp.bfloat16):
    array = deviation * jax.random.normal(stream_key, dims, jnp.float32)
    if cuts:
        array = array * block_scale(stream_key, dims, cuts, -0.22, 0.18)
    return jnp.clip(array, -most, most).astype(kind)


def setup_inputs(seed: int = 0) -> dict:
    arg_keys = jax.random.split(jax.random.key(seed), 9)
    return {
        "hidden": gaussian(arg_keys[0], (TOKENS, D), 1.0, 6.0, ((0, 32),)),
        "targets": draw_targets(jax.random.fold_in(arg_keys[8], 71), 0),
        "input_ids": draw_input_ids(jax.random.fold_in(arg_keys[8], 71), 0),
        "input_grads": gaussian(arg_keys[3], (TOKENS, D), 0.02, 0.3125, ((0, 32),)),
        "table": gaussian(arg_keys[4], (VOCAB, D), (D // 64) ** -0.5, 0.75, ((0, 16), (1, 2))),
        "keep": draw_keep(jax.random.fold_in(arg_keys[8], 71), 0),
        "first_moment": gaussian(arg_keys[6], (VOCAB, D), 0.001, 0.015625, ((0, 16), (1, 2))),
        "second_moment": jnp.clip(jnp.exp(math.log(9.953975677490234e-06) - 2.2995956 * jax.random.uniform(arg_keys[7], (VOCAB, D), jnp.float32) ** block_scale(arg_keys[7], (VOCAB, D), ((0, 16), (1, 2)), -0.2, 0.2)), 9.98377799987793e-07, 9.953975677490234e-06).astype(jnp.bfloat16),
    }


SOFTCAP = 30.0
LEARN = 0.01
EPSILON = 1e-08

def reference(hidden, targets, input_ids, input_grads, table, keep, first_moment, second_moment):
    raw = lax.dot_general(hidden, table, (((1,), (1,)), ((), ())), preferred_element_type=jnp.float32)
    capped = SOFTCAP * jnp.tanh(raw / SOFTCAP)
    keepf = keep.astype(jnp.float32)
    weights = jnp.exp(capped) * keepf[None, :]
    total = lax.optimization_barrier(jnp.sum(weights, axis=1))
    columns = jnp.arange(VOCAB, dtype=jnp.int32)
    onehot = (targets[:, None] == columns[None, :]).astype(jnp.float32)
    target_logit = lax.optimization_barrier(jnp.sum(capped * onehot, axis=1))
    loss = jnp.sum(jnp.log(total) - target_logit)
    slope = 1.0 - (capped / SOFTCAP) ** 2
    dlogits = ((weights / total[:, None] - onehot) * slope).astype(jnp.bfloat16)
    head_grad = lax.dot_general(dlogits, hidden, (((0,), (0,)), ((), ())), preferred_element_type=jnp.float32)
    row_grad = jax.ops.segment_sum(input_grads.astype(jnp.float32), input_ids, num_segments=VOCAB)
    grad = head_grad + math.sqrt(D) * row_grad
    kept = keep[:, None] > 0
    first_new = (0.9 * first_moment.astype(jnp.float32) + 0.1 * grad).astype(jnp.bfloat16)
    second_new = (0.95 * second_moment.astype(jnp.float32) + 0.05 * grad * grad).astype(jnp.bfloat16)
    corr_one = 1.0 - 0.9 ** 10
    corr_two = 1.0 - 0.95 ** 10
    update = first_new.astype(jnp.float32) / corr_one / (jnp.sqrt(second_new.astype(jnp.float32) / corr_two) + EPSILON)
    table_new = (table.astype(jnp.float32) - LEARN * update).astype(jnp.bfloat16)
    new_table = jnp.where(kept, table_new, table)
    new_first = jnp.where(kept, first_new, first_moment)
    new_second = jnp.where(kept, second_new, second_moment)
    return (new_table, new_first, new_second, loss)
```

```python
import math

import jax
import jax.numpy as jnp
from jax import lax
from jax.sharding import PartitionSpec as P

SOFTCAP = 30.0
LEARN = 0.01
EPSILON = 1e-08


def contract_last(left, right):
    return lax.dot_general(
        left, right, (((1,), (1,)), ((), ())), preferred_element_type=jnp.float32
    )


def contract_first(left, right):
    return lax.dot_general(
        left, right, (((0,), (0,)), ((), ())), preferred_element_type=jnp.float32
    )


def body(hidden, targets, input_ids, input_grads, table, keep, first_moment, second_moment):
    rows_here = table.shape[0]
    row_start = lax.axis_index(("pipe", "vocab")) * rows_here
    keepf = keep.astype(jnp.float32)
    scale = math.sqrt(hidden.shape[1])
    groups_dp = lax.axis_size("dp")
    row_iota = jnp.arange(rows_here, dtype=jnp.int32)
    both = jnp.stack([targets, input_ids])
    packed = lax.all_to_all(
        jnp.stack([hidden, input_grads]), "dp", split_axis=2, concat_axis=1, tiled=True
    )
    ids_all = lax.all_gather(both, ("pipe", "vocab", "dp"), axis=1, tiled=True)
    tokens_all = lax.all_gather(packed[0], ("pipe", "vocab"), axis=0, tiled=True)
    grads_all = lax.all_gather(packed[1], ("pipe", "vocab"), axis=0, tiled=True)
    tokens = tokens_all.shape[0]
    share = tokens // groups_dp
    start = lax.axis_index("dp") * share
    goals = lax.dynamic_slice(ids_all[0], (start,), (share,))
    raw = lax.psum_scatter(
        contract_last(tokens_all, table), "dp", scatter_dimension=0, tiled=True
    )
    capped = SOFTCAP * jnp.tanh(raw / SOFTCAP)
    onehot = ((goals - row_start)[:, None] == row_iota[None, :]).astype(jnp.float32)
    weights = jnp.exp(capped) * keepf[None, :]
    local = jnp.stack([jnp.sum(weights, axis=1), jnp.sum(capped * onehot, axis=1)])
    placed = lax.dynamic_update_slice(jnp.zeros((2, tokens), jnp.float32), local, (0, start))
    sums = lax.psum(placed, ("pipe", "dp", "vocab"))
    token_loss = jnp.sum(jnp.log(sums[0]) - sums[1])
    total = lax.dynamic_slice(sums[0], (start,), (share,))
    slope = 1.0 - (capped / SOFTCAP) ** 2
    dlogits = ((weights / total[:, None] - onehot) * slope).astype(jnp.bfloat16)
    dlogits = lax.all_gather(dlogits, "dp", axis=0, tiled=True)
    selector = ((ids_all[1] - row_start)[None, :] == row_iota[:, None]).astype(jnp.bfloat16)
    finished = contract_first(dlogits, tokens_all) + scale * jnp.dot(
        selector, grads_all, preferred_element_type=jnp.float32
    )
    kept = keep[:, None] > 0
    first_new = (0.9 * first_moment.astype(jnp.float32) + 0.1 * finished).astype(jnp.bfloat16)
    second_new = (0.95 * second_moment.astype(jnp.float32) + 0.05 * finished * finished).astype(
        jnp.bfloat16
    )
    corr_one = 1.0 - 0.9**10
    corr_two = 1.0 - 0.95**10
    update = (
        first_new.astype(jnp.float32)
        / corr_one
        / (jnp.sqrt(second_new.astype(jnp.float32) / corr_two) + EPSILON)
    )
    table_new = (table.astype(jnp.float32) - LEARN * update).astype(jnp.bfloat16)
    new_table = jnp.where(kept, table_new, table)
    new_first = jnp.where(kept, first_new, first_moment)
    new_second = jnp.where(kept, second_new, second_moment)
    return (new_table, new_first, new_second, token_loss)


def solution(mesh):
    placed = (
        P(("pipe", "dp", "vocab"), None),
        P(("pipe", "dp", "vocab")),
        P(("pipe", "dp", "vocab")),
        P(("pipe", "dp", "vocab"), None),
        P(("pipe", "vocab"), "dp"),
        P(("pipe", "vocab")),
        P(("pipe", "vocab"), "dp"),
        P(("pipe", "vocab"), "dp"),
    )
    return jax.shard_map(
        body,
        mesh=mesh,
        in_specs=placed,
        out_specs=(
            P(("pipe", "vocab"), "dp"),
            P(("pipe", "vocab"), "dp"),
            P(("pipe", "vocab"), "dp"),
            P(),
        ),
        check_vma=False,
    )
```

```python
import functools
import math

import jax
import jax.numpy as jnp
from jax import lax
from jax.experimental import pallas as pl
from jax.experimental.pallas import tpu as pltpu
from jax.sharding import PartitionSpec as P

SOFTCAP = 30.0
LEARN = 0.01
EPSILON = 1e-08
MESH = pl.DeviceIdType.MESH
CHUNK = 256
VMEM_LIMIT = 56 * 2**20


def chunk_rows(c):
    return pl.ds(c * CHUNK, CHUNK)


class Gather:
    def __init__(self, place, buf, stage, y_send, y_recv, send, recv):
        self.n_pipe, self.n_vocab, self.pipe, self.dp, self.vocab = place
        self.n_x = self.n_pipe // 2
        self.x, self.core = self.pipe // 2, self.pipe % 2
        self.buf, self.stage = buf, stage
        self.y_send, self.y_recv, self.send, self.recv = y_send, y_recv, send, recv
        self.rows = stage.shape[0]
        self.started = []

    def pipe_of(self, k):
        return ((self.x + k) % self.n_x) * 2 + self.core

    def origin(self, k):
        return ((self.x + self.n_x - k) % self.n_x) * 2 + self.core

    def vocab_of(self, k):
        return (self.vocab + k) % self.n_vocab

    def vocab_origin(self, k):
        return (self.vocab + self.n_vocab - k) % self.n_vocab

    def sibling(self):
        return self.pipe + 1 - 2 * self.core

    def own(self, dp):
        block = self.pipe * self.n_vocab + self.vocab
        return pl.ds(pl.multiple_of((block * 2 + dp) * self.rows, self.rows), self.rows)

    def copy(self, pipe, vocab, slot, dest, device):
        block = pipe * self.n_vocab + vocab
        size = 2 * self.rows
        part = self.buf.at[pl.ds(pl.multiple_of(block * size, size), size)]
        return pltpu.make_async_remote_copy(
            src_ref=part, dst_ref=part,
            send_sem=self.send.at[slot, dest], recv_sem=self.recv.at[block],
            device_id=device, device_id_type=MESH,
        )

    def start(self, pipe, vocab, slot, dest, device):
        copy = self.copy(pipe, vocab, slot, dest, device)
        copy.start()
        self.started.append(copy)

    def pair_copy(self):
        return pltpu.make_async_remote_copy(
            src_ref=self.stage, dst_ref=self.buf.at[self.own(self.dp)],
            send_sem=self.y_send, recv_sem=self.y_recv,
            device_id={"dp": 1 - self.dp}, device_id_type=MESH,
        )

    def pair(self):
        copy = self.pair_copy()
        copy.start()
        self.first = copy

    def to_x(self, pipe, vocab, slot):
        for k in range(1, self.n_x):
            self.start(pipe, vocab, slot, self.n_vocab - 2 + k, {"pipe": self.pipe_of(k)})

    def to_core(self, pipe, vocab, slot):
        dest = self.n_vocab + self.n_x - 2
        self.start(pipe, vocab, slot, dest, {"pipe": self.sibling()})

    def arrived(self, pipe, vocab):
        self.copy(pipe, vocab, 0, 0, {"pipe": self.sibling()}).wait_recv()

    def spread(self):
        self.first.wait_recv()
        self.to_x(self.pipe, self.vocab, 0)
        for k in range(1, self.n_vocab):
            self.start(self.pipe, self.vocab, 0, k - 1, {"vocab": self.vocab_of(k)})
        self.to_core(self.pipe, self.vocab, 0)

    def relay(self):
        for k in range(1, self.n_vocab):
            source = self.vocab_origin(k)
            self.arrived(self.pipe, source)
            self.to_x(self.pipe, source, k)
            self.to_core(self.pipe, source, k)
        for j in range(1, self.n_x):
            for k in range(self.n_vocab):
                pipe, source = self.origin(j), self.vocab_origin(k)
                self.arrived(pipe, source)
                self.to_core(pipe, source, j * self.n_vocab + k)

    def finish(self):
        for j in range(self.n_x):
            for k in range(self.n_vocab):
                pipe = self.origin(j) + 1 - 2 * self.core
                self.arrived(pipe, self.vocab_origin(k))

    def sent(self):
        self.first.wait_send()
        for copy in self.started:
            copy.wait_send()


def head_kernel(
    n_pipe, n_vocab, hid, grd, meta, keep, table_hbm,
    hbuf, gbuf, dlog, ids, loss,
    table, hstage, gstage, goals, outgoing, incoming, logits, v_sum, x_sum, c_sum, losses,
    table_sem, hy_send, hy_recv, h_send, h_recv, gy_send, gy_recv, g_send, g_recv,
    l_send, l_recv, d_send, d_recv, vs_send, vs_recv, xs_send, xs_recv, one_send, one_recv,
):
    pipe, dp, vocab = lax.axis_index("pipe"), lax.axis_index("dp"), lax.axis_index("vocab")
    place = (n_pipe, n_vocab, pipe, dp, vocab)
    other = 1 - dp
    vr, half = table.shape
    share = outgoing.shape[1]
    chunks = vr // CHUNK
    row_start = (pipe * n_vocab + vocab) * vr

    load = pltpu.make_async_copy(table_hbm, table, table_sem)
    load.start()
    h = Gather(place, hbuf, hstage, hy_send, hy_recv, h_send, h_recv)
    g = Gather(place, gbuf, gstage, gy_send, gy_recv, g_send, g_recv)

    barrier = pltpu.get_barrier_semaphore()
    peers = [{"dp": other}, {"pipe": h.sibling()}]
    peers += [{"vocab": h.vocab_of(k)} for k in range(1, n_vocab)]
    peers += [{"pipe": h.pipe_of(k)} for k in range(1, h.n_x)]
    for peer in peers:
        pl.semaphore_signal(barrier, inc=1, device_id=peer, device_id_type=MESH)

    mine = pl.ds(pl.multiple_of(dp * half, 128), half)
    theirs = pl.ds(pl.multiple_of(other * half, 128), half)
    hstage[:, :half] = hid[:, theirs]
    hstage[:, half:] = meta[...]
    hbuf[h.own(dp), :half] = hid[:, mine]
    hbuf[h.own(dp), half:] = meta[...]
    gstage[...] = grd[:, theirs]
    gbuf[g.own(dp), :] = grd[:, mine]
    pl.semaphore_wait(barrier, len(peers))

    h.pair()
    g.pair()
    h.spread()
    h.relay()
    h.finish()
    g.spread()

    spots = hbuf[:, half:].astype(jnp.float32).T
    goals[...] = jnp.broadcast_to(
        (spots[0:1] * 256.0 + spots[1:2]).astype(jnp.int32) - row_start, goals.shape
    )
    ids[...] = jnp.broadcast_to(
        (spots[2:3] * 256.0 + spots[3:4]).astype(jnp.int32) - row_start, ids.shape
    )
    load.wait()

    def partial(c, which):
        tokens = pl.ds(pl.multiple_of(which * share, share), share)
        return lax.dot_general(
            table[chunk_rows(c), :], hbuf[tokens, :half],
            (((1,), (1,)), ((), ())), preferred_element_type=jnp.float32,
        )

    def exchange(source, dest, send_sem, recv_sem, device):
        return pltpu.make_async_remote_copy(
            src_ref=source, dst_ref=dest, send_sem=send_sem, recv_sem=recv_sem,
            device_id=device, device_id_type=MESH,
        )

    logit_copies = []
    for c in range(chunks):
        outgoing[chunk_rows(c), :] = partial(c, other)
        copy = exchange(
            outgoing.at[chunk_rows(c)], incoming.at[chunk_rows(c)],
            l_send.at[c], l_recv.at[c], {"dp": other},
        )
        copy.start()
        logit_copies.append(copy)
    for c in range(chunks):
        logits[chunk_rows(c), :] = partial(c, dp)
    g.relay()

    goal = goals[0:1, pl.ds(pl.multiple_of(dp * share, share), share)]
    row_iota = lax.broadcasted_iota(jnp.int32, (CHUNK, share), 0)
    total = jnp.zeros((1, share), jnp.float32)
    target = jnp.zeros((1, share), jnp.float32)
    for c in range(chunks):
        logit_copies[c].wait_recv()
        rows = chunk_rows(c)
        unit = jnp.tanh((logits[rows, :] + incoming[rows, :]) * (1.0 / SOFTCAP))
        capped = SOFTCAP * unit
        weights = jnp.exp(capped) * keep[rows, :]
        hit = row_iota == goal - c * CHUNK
        total += jnp.sum(weights, axis=0, keepdims=True)
        target += jnp.sum(jnp.where(hit, capped, 0.0), axis=0, keepdims=True)
        logits[rows, :] = unit
        incoming[rows, :] = weights

    small = []

    def summed(slots, index, count, offsets, peer, send, recv):
        for k in offsets:
            copy = exchange(slots.at[index], slots.at[index], send.at[k], recv.at[index], peer(k))
            copy.start()
            small.append(copy)
        for k in offsets:
            source = (index + count - k) % count
            exchange(
                slots.at[source], slots.at[source], send.at[k], recv.at[source], peer(k)
            ).wait_recv()
        value = slots[0]
        for k in range(1, count):
            value = value + slots[k]
        return value

    v_sum[vocab, 0:1] = total
    v_sum[vocab, 1:2] = target
    v_sum[vocab, 2:8] = jnp.zeros((6, share), jnp.float32)
    x_sum[h.x] = summed(
        v_sum, vocab, n_vocab, range(1, n_vocab),
        lambda k: {"vocab": h.vocab_of(k)}, vs_send, vs_recv,
    )
    c_sum[h.core] = summed(
        x_sum, h.x, h.n_x, range(1, h.n_x),
        lambda k: {"pipe": h.pipe_of(k)}, xs_send, xs_recv,
    )
    sums = summed(
        c_sum, h.core, 2, range(1, 2),
        lambda k: {"pipe": h.sibling()}, one_send, one_recv,
    )
    total, target = sums[0:1], sums[1:2]
    inverse = 1.0 / total
    dlogit_copies = []
    for c in range(chunks):
        rows = chunk_rows(c)
        unit = logits[rows, :]
        hit = row_iota == goal - c * CHUNK
        slope = 1.0 - unit * unit
        value = (incoming[rows, :] * inverse - jnp.where(hit, 1.0, 0.0)) * slope
        dlog[dp, rows, :] = value.astype(jnp.bfloat16)
        part = dlog.at[dp, rows]
        copy = exchange(part, part, d_send.at[c], d_recv.at[c], {"dp": other})
        copy.start()
        dlogit_copies.append(copy)
    piece = jnp.sum(jnp.log(total) - target, axis=1, keepdims=True)
    losses[dp] = jnp.broadcast_to(piece, losses.shape[1:])
    part = losses.at[dp]
    copy = exchange(part, part, one_send.at[2], one_recv.at[2], {"dp": other})
    copy.start()
    g.finish()
    copy.wait()
    loss[...] = losses[0] + losses[1]
    for copy in dlogit_copies:
        copy.wait()
    for copy in logit_copies + small:
        copy.wait_send()
    h.sent()
    g.sent()


def adam_kernel(scale, dlog, tokens, grads, ids, keep, table, first, second, *outs):
    new_table, new_first, new_second = outs
    rows, width = table.shape
    share = dlog.shape[2]
    row_iota = lax.broadcasted_iota(jnp.int32, (rows, ids.shape[1]), 0)
    here = row_iota + pl.program_id(0) * rows
    selector = jnp.where(ids[0:1, :] == here, 1.0, 0.0).astype(jnp.bfloat16)
    kept = keep[...] > 0.0
    corr_one = 1.0 - 0.9**10
    corr_two = 1.0 - 0.95**10
    step = math.gcd(width, 768)
    for at in range(0, width, step):
        cols = slice(at, at + step)
        grad = scale * jnp.dot(selector, grads[:, cols], preferred_element_type=jnp.float32)
        for j in range(2):
            grad += jnp.dot(
                dlog[j], tokens[j * share:(j + 1) * share, cols],
                preferred_element_type=jnp.float32,
            )
        m1, m2, old = first[:, cols], second[:, cols], table[:, cols]
        f_new = (0.9 * m1.astype(jnp.float32) + 0.1 * grad).astype(jnp.bfloat16)
        s_new = (0.95 * m2.astype(jnp.float32) + 0.05 * grad * grad).astype(jnp.bfloat16)
        root = jnp.sqrt(s_new.astype(jnp.float32) * (1.0 / corr_two)) + EPSILON
        update = f_new.astype(jnp.float32) * (LEARN / corr_one) / root
        t_new = (old.astype(jnp.float32) - update).astype(jnp.bfloat16)
        new_table[:, cols] = jnp.where(kept, t_new, old)
        new_first[:, cols] = jnp.where(kept, f_new, m1)
        new_second[:, cols] = jnp.where(kept, s_new, m2)


def body(hidden, targets, input_ids, input_grads, table, keep, first_moment, second_moment):
    n_pipe, n_vocab = lax.axis_size("pipe"), lax.axis_size("vocab")
    n_x = n_pipe // 2
    here, width = hidden.shape
    vr, half = table.shape
    count = here * 2 * n_pipe * n_vocab
    share = count // 2
    chunks = vr // CHUNK
    meta = jnp.stack(
        [targets // 256, targets % 256, input_ids // 256, input_ids % 256], axis=1
    ).astype(jnp.bfloat16)
    meta = jnp.pad(meta, ((0, 0), (0, 124)))
    keep_col = keep.astype(jnp.float32)[:, None]
    bf16, f32 = jnp.bfloat16, jnp.float32
    vmem = pl.BlockSpec(memory_space=pltpu.VMEM)
    dma = pltpu.SemaphoreType.DMA
    dests = n_vocab + n_x - 1
    tokens, grads, dlog, ids, loss = pl.pallas_call(
        functools.partial(head_kernel, n_pipe, n_vocab),
        out_shape=(
            jax.ShapeDtypeStruct((count, half + 128), bf16),
            jax.ShapeDtypeStruct((count, half), bf16),
            jax.ShapeDtypeStruct((2, vr, share), bf16),
            jax.ShapeDtypeStruct((8, count), jnp.int32),
            jax.ShapeDtypeStruct((8, 128), f32),
        ),
        in_specs=[vmem] * 4 + [pl.BlockSpec(memory_space=pl.ANY)],
        out_specs=(vmem,) * 5,
        scratch_shapes=[
            pltpu.VMEM((vr, half), bf16),
            pltpu.VMEM((here, half + 128), bf16),
            pltpu.VMEM((here, half), bf16),
            pltpu.VMEM((8, count), jnp.int32),
            pltpu.VMEM((vr, share), f32),
            pltpu.VMEM((vr, share), f32),
            pltpu.VMEM((vr, share), f32),
            pltpu.VMEM((n_vocab, 8, share), f32),
            pltpu.VMEM((n_x, 8, share), f32),
            pltpu.VMEM((2, 8, share), f32),
            pltpu.VMEM((2, 8, 128), f32),
            dma,
            dma, dma, dma((n_x * n_vocab, dests)), dma((n_pipe * n_vocab,)),
            dma, dma, dma((n_x * n_vocab, dests)), dma((n_pipe * n_vocab,)),
            dma((chunks,)), dma((chunks,)), dma((chunks,)), dma((chunks,)),
            dma((n_vocab,)), dma((n_vocab,)), dma((n_x,)), dma((n_x,)), dma((3,)), dma((3,)),
        ],
        compiler_params=pltpu.CompilerParams(
            collective_id=0, has_side_effects=True, vmem_limit_bytes=VMEM_LIMIT
        ),
        cost_estimate=pl.CostEstimate(
            flops=2 * count * vr * half, bytes_accessed=2 * vr * half, transcendentals=0
        ),
    )(hidden, input_grads, meta, keep_col, table)

    once = pl.Buffered(buffer_count=1)
    tile = pl.BlockSpec((CHUNK, half), lambda i: (i, 0))
    new_table, new_first, new_second = pl.pallas_call(
        functools.partial(adam_kernel, math.sqrt(width)),
        out_shape=(jax.ShapeDtypeStruct((vr, half), bf16),) * 3,
        grid=(chunks,),
        in_specs=[
            pl.BlockSpec((2, CHUNK, share), lambda i: (0, i, 0)),
            pl.BlockSpec((count, half), lambda i: (0, 0), pipeline_mode=once),
            pl.BlockSpec((count, half), lambda i: (0, 0), pipeline_mode=once),
            pl.BlockSpec((8, count), lambda i: (0, 0)),
            pl.BlockSpec((CHUNK, 1), lambda i: (i, 0)),
            tile, tile, tile,
        ],
        out_specs=(tile,) * 3,
        compiler_params=pltpu.CompilerParams(vmem_limit_bytes=VMEM_LIMIT),
        cost_estimate=pl.CostEstimate(
            flops=4 * count * vr * half, bytes_accessed=12 * vr * half, transcendentals=0
        ),
    )(dlog, tokens, grads, ids, keep_col, table, first_moment, second_moment)
    return (new_table, new_first, new_second, loss[0, 0])


def solution(mesh):
    placed = (
        P(("pipe", "dp", "vocab"), None),
        P(("pipe", "dp", "vocab")),
        P(("pipe", "dp", "vocab")),
        P(("pipe", "dp", "vocab"), None),
        P(("pipe", "vocab"), "dp"),
        P(("pipe", "vocab")),
        P(("pipe", "vocab"), "dp"),
        P(("pipe", "vocab"), "dp"),
    )
    return jax.shard_map(
        body,
        mesh=mesh,
        in_specs=placed,
        out_specs=(
            P(("pipe", "vocab"), "dp"),
            P(("pipe", "vocab"), "dp"),
            P(("pipe", "vocab"), "dp"),
            P(),
        ),
        check_vma=False,
    )
```

```python
import functools
import math

import jax
import jax.numpy as jnp
from jax import lax
from jax.experimental import pallas as pl
from jax.experimental.pallas import tpu as pltpu
from jax.sharding import PartitionSpec as P

SOFTCAP = 30.0
LEARN = 0.01
EPSILON = 1e-08
MESH = pl.DeviceIdType.MESH
CHUNK = 256
VMEM_LIMIT = 56 * 2**20


def chunk_rows(c):
    return pl.ds(c * CHUNK, CHUNK)


def row_to_column(row):
    wide = jnp.broadcast_to(row[...].astype(jnp.float32), (8, row.shape[1]))
    return wide.T[:, 0:1]


def id_columns(targets, input_ids):
    count = targets.shape[1]
    square = lax.broadcasted_iota(jnp.int32, (count, count), 0) == lax.broadcasted_iota(
        jnp.int32, (count, count), 1
    )
    lane = lax.broadcasted_iota(jnp.int32, (count, 128), 1)
    result = jnp.zeros((count, 128), jnp.float32)
    rows = [targets[...] >> 8, targets[...] & 255, input_ids[...] >> 8, input_ids[...] & 255]
    for at, row in enumerate(rows):
        column = jnp.sum(
            jnp.where(square, row.astype(jnp.float32), 0.0), axis=1, keepdims=True
        )
        result = jnp.where(lane == at, column, result)
    return result.astype(jnp.bfloat16)


class Gather:
    def __init__(self, place, buf, stage, y_send, y_recv, send, recv):
        self.n_pipe, self.n_vocab, self.pipe, self.dp, self.vocab = place
        self.n_x = self.n_pipe // 2
        self.x, self.core = self.pipe // 2, self.pipe % 2
        self.buf, self.stage = buf, stage
        self.y_send, self.y_recv, self.send, self.recv = y_send, y_recv, send, recv
        self.rows = stage.shape[0]
        self.started = []

    def pipe_of(self, k):
        return ((self.x + k) % self.n_x) * 2 + self.core

    def origin(self, k):
        return ((self.x + self.n_x - k) % self.n_x) * 2 + self.core

    def vocab_of(self, k):
        return (self.vocab + k) % self.n_vocab

    def vocab_origin(self, k):
        return (self.vocab + self.n_vocab - k) % self.n_vocab

    def sibling(self):
        return self.pipe + 1 - 2 * self.core

    def block(self, pipe, vocab):
        return (pipe % 2 * self.n_x + pipe // 2) * self.n_vocab + vocab

    def own(self, dp):
        block = self.block(self.pipe, self.vocab)
        return pl.ds(pl.multiple_of((block * 2 + dp) * self.rows, self.rows), self.rows)

    def copy(self, pipe, vocab, slot, dest, device):
        block = self.block(pipe, vocab)
        size = 2 * self.rows
        part = self.buf.at[pl.ds(pl.multiple_of(block * size, size), size)]
        return pltpu.make_async_remote_copy(
            src_ref=part, dst_ref=part,
            send_sem=self.send.at[slot, dest], recv_sem=self.recv.at[block],
            device_id=device, device_id_type=MESH,
        )

    def start(self, pipe, vocab, slot, dest, device):
        copy = self.copy(pipe, vocab, slot, dest, device)
        copy.start()
        self.started.append(copy)

    def pair_copy(self):
        return pltpu.make_async_remote_copy(
            src_ref=self.stage, dst_ref=self.buf.at[self.own(self.dp)],
            send_sem=self.y_send, recv_sem=self.y_recv,
            device_id={"dp": 1 - self.dp}, device_id_type=MESH,
        )

    def pair(self):
        copy = self.pair_copy()
        copy.start()
        self.first = copy

    def to_x(self, pipe, vocab, slot):
        for k in range(1, self.n_x):
            self.start(pipe, vocab, slot, self.n_vocab - 2 + k, {"pipe": self.pipe_of(k)})

    def to_core(self, pipe, vocab, slot):
        dest = self.n_vocab + self.n_x - 2
        self.start(pipe, vocab, slot, dest, {"pipe": self.sibling()})

    def arrived(self, pipe, vocab):
        self.copy(pipe, vocab, 0, 0, {"pipe": self.sibling()}).wait_recv()

    def spread(self):
        self.first.wait_recv()
        self.to_x(self.pipe, self.vocab, 0)
        for k in range(1, self.n_vocab):
            self.start(self.pipe, self.vocab, 0, k - 1, {"vocab": self.vocab_of(k)})
        self.to_core(self.pipe, self.vocab, 0)

    def relay_near(self):
        for k in range(1, self.n_vocab):
            source = self.vocab_origin(k)
            self.arrived(self.pipe, source)
            self.to_x(self.pipe, source, k)
            self.to_core(self.pipe, source, k)

    def relay_far(self, j):
        for k in range(self.n_vocab):
            pipe, source = self.origin(j), self.vocab_origin(k)
            self.arrived(pipe, source)
            self.to_core(pipe, source, j * self.n_vocab + k)

    def finish(self, j):
        for k in range(self.n_vocab):
            pipe = self.origin(j) + 1 - 2 * self.core
            self.arrived(pipe, self.vocab_origin(k))

    def sent(self):
        self.first.wait_send()
        for copy in self.started:
            copy.wait_send()


def head_kernel(
    n_pipe, n_vocab, hid, grd, aims, reads, keep_row, table_hbm,
    hbuf, gbuf, dlog, ids, loss,
    table, keep, hstage, gstage, goals, outgoing, incoming, logits, v_sum, x_sum, c_sum, losses,
    table_sem, hy_send, hy_recv, h_send, h_recv, gy_send, gy_recv, g_send, g_recv,
    l_send, l_recv, d_send, d_recv, vs_send, vs_recv, xs_send, xs_recv, one_send, one_recv,
):
    pipe, dp, vocab = lax.axis_index("pipe"), lax.axis_index("dp"), lax.axis_index("vocab")
    place = (n_pipe, n_vocab, pipe, dp, vocab)
    other = 1 - dp
    vr, half = table.shape
    share = outgoing.shape[1]
    chunks = vr // CHUNK
    row_start = (pipe * n_vocab + vocab) * vr

    load = pltpu.make_async_copy(table_hbm, table, table_sem)
    load.start()
    h = Gather(place, hbuf, hstage, hy_send, hy_recv, h_send, h_recv)
    g = Gather(place, gbuf, gstage, gy_send, gy_recv, g_send, g_recv)

    barrier = pltpu.get_barrier_semaphore()
    peers = [{"dp": other}, {"pipe": h.sibling()}]
    peers += [{"vocab": h.vocab_of(k)} for k in range(1, n_vocab)]
    peers += [{"pipe": h.pipe_of(k)} for k in range(1, h.n_x)]
    for peer in peers:
        pl.semaphore_signal(barrier, inc=1, device_id=peer, device_id_type=MESH)

    mine = pl.ds(pl.multiple_of(dp * half, 128), half)
    theirs = pl.ds(pl.multiple_of(other * half, 128), half)
    hstage[:, :half] = hid[:, theirs]
    meta = id_columns(aims, reads)
    hstage[:, half:] = meta
    hbuf[h.own(dp), :half] = hid[:, mine]
    hbuf[h.own(dp), half:] = meta
    gstage[...] = grd[:, theirs]
    gbuf[g.own(dp), :] = grd[:, mine]
    pl.semaphore_wait(barrier, len(peers))

    h.pair()
    g.pair()
    h.spread()
    keep[...] = row_to_column(keep_row)
    h.relay_near()
    load.wait()

    group = share // h.n_x

    def partial(c, which, x):
        start = pl.multiple_of(which * share + x * group, group)
        return lax.dot_general(
            table[chunk_rows(c), :], hbuf[pl.ds(start, group), :half],
            (((1,), (1,)), ((), ())), preferred_element_type=jnp.float32,
        )

    def exchange(source, dest, send_sem, recv_sem, device):
        return pltpu.make_async_remote_copy(
            src_ref=source, dst_ref=dest, send_sem=send_sem, recv_sem=recv_sem,
            device_id=device, device_id_type=MESH,
        )

    logit_copies = []
    for j in range(h.n_x):
        if j:
            h.relay_far(j)
        h.finish(j)
        if j == h.n_x - 1:
            g.spread()
        x = h.origin(j) // 2
        lanes = pl.ds(pl.multiple_of(x * group, group), group)
        for c in range(chunks):
            rows = chunk_rows(c)
            outgoing[rows, lanes] = partial(c, other, x)
            copy = exchange(
                outgoing.at[rows, lanes], incoming.at[rows, lanes],
                l_send.at[c, x], l_recv.at[c, x], {"dp": other},
            )
            copy.start()
            logit_copies.append(copy)
        for c in range(chunks):
            logits[chunk_rows(c), lanes] = partial(c, dp, x)
    spots = hbuf[:, half:].astype(jnp.float32).T
    goals[...] = jnp.broadcast_to(
        (spots[0:1] * 256.0 + spots[1:2]).astype(jnp.int32) - row_start, goals.shape
    )
    ids[...] = jnp.broadcast_to(
        (spots[2:3] * 256.0 + spots[3:4]).astype(jnp.int32) - row_start, ids.shape
    )
    g.relay_near()
    for j in range(1, g.n_x):
        g.relay_far(j)

    goal = goals[0:1, pl.ds(pl.multiple_of(dp * share, share), share)]
    row_iota = lax.broadcasted_iota(jnp.int32, (CHUNK, share), 0)
    total = jnp.zeros((1, share), jnp.float32)
    target = jnp.zeros((1, share), jnp.float32)
    for c in range(chunks):
        rows = chunk_rows(c)
        for x in range(h.n_x):
            lanes = pl.ds(x * group, group)
            exchange(
                outgoing.at[rows, lanes], incoming.at[rows, lanes],
                l_send.at[c, x], l_recv.at[c, x], {"dp": other},
            ).wait_recv()
        unit = jnp.tanh((logits[rows, :] + incoming[rows, :]) * (1.0 / SOFTCAP))
        capped = SOFTCAP * unit
        weights = jnp.exp(capped) * keep[rows, :]
        hit = row_iota == goal - c * CHUNK
        total += jnp.sum(weights, axis=0, keepdims=True)
        target += jnp.sum(jnp.where(hit, capped, 0.0), axis=0, keepdims=True)
        logits[rows, :] = unit
        incoming[rows, :] = weights

    small = []

    def summed(slots, index, count, offsets, peer, send, recv):
        for k in offsets:
            copy = exchange(slots.at[index], slots.at[index], send.at[k], recv.at[index], peer(k))
            copy.start()
            small.append(copy)
        for k in offsets:
            source = (index + count - k) % count
            exchange(
                slots.at[source], slots.at[source], send.at[k], recv.at[source], peer(k)
            ).wait_recv()
        value = slots[0]
        for k in range(1, count):
            value = value + slots[k]
        return value

    v_sum[vocab, 0:1] = total
    v_sum[vocab, 1:2] = target
    v_sum[vocab, 2:8] = jnp.zeros((6, share), jnp.float32)
    x_sum[h.x] = summed(
        v_sum, vocab, n_vocab, range(1, n_vocab),
        lambda k: {"vocab": h.vocab_of(k)}, vs_send, vs_recv,
    )
    c_sum[h.core] = summed(
        x_sum, h.x, h.n_x, range(1, h.n_x),
        lambda k: {"pipe": h.pipe_of(k)}, xs_send, xs_recv,
    )
    sums = summed(
        c_sum, h.core, 2, range(1, 2),
        lambda k: {"pipe": h.sibling()}, one_send, one_recv,
    )
    total, target = sums[0:1], sums[1:2]
    inverse = 1.0 / total
    dlogit_copies = []
    for c in range(chunks):
        rows = chunk_rows(c)
        unit = logits[rows, :]
        hit = row_iota == goal - c * CHUNK
        slope = 1.0 - unit * unit
        value = (incoming[rows, :] * inverse - jnp.where(hit, 1.0, 0.0)) * slope
        dlog[dp, rows, :] = value.astype(jnp.bfloat16)
        part = dlog.at[dp, rows]
        copy = exchange(part, part, d_send.at[c], d_recv.at[c], {"dp": other})
        copy.start()
        dlogit_copies.append(copy)
    piece = jnp.sum(jnp.log(total) - target, axis=1, keepdims=True)
    losses[dp] = jnp.broadcast_to(piece, losses.shape[1:])
    part = losses.at[dp]
    copy = exchange(part, part, one_send.at[2], one_recv.at[2], {"dp": other})
    copy.start()
    for j in range(g.n_x):
        g.finish(j)
    copy.wait()
    loss[...] = losses[0, 0:1, 0:1] + losses[1, 0:1, 0:1]
    for copy in dlogit_copies:
        copy.wait()
    for copy in logit_copies + small:
        copy.wait_send()
    h.sent()
    g.sent()


def adam_kernel(scale, dlog, tokens, grads, ids, keep, table, first, second, *rest):
    new_table, new_first, new_second, selector, kept_column = rest
    share = dlog.shape[2]

    @pl.when(pl.program_id(0) == 0)
    def _():
        row_iota = lax.broadcasted_iota(jnp.int32, selector.shape, 0)
        hit = ids[0:1, :] == row_iota
        selector[...] = jnp.where(hit, 1.0, 0.0).astype(jnp.bfloat16)
        kept_column[...] = row_to_column(keep)

    corr_one = 1.0 - 0.9**10
    corr_two = 1.0 - 0.95**10
    for c in range(table.shape[0] // CHUNK):
        rows = chunk_rows(c)
        kept = kept_column[rows, :] > 0.0
        grad = scale * jnp.dot(
            selector[rows, :], grads[...], preferred_element_type=jnp.float32
        )
        for j in range(2):
            grad += jnp.dot(
                dlog[j, rows, :], tokens[j * share:(j + 1) * share, :],
                preferred_element_type=jnp.float32,
            )
        m1, m2, old = first[rows, :], second[rows, :], table[rows, :]
        f_new = (0.9 * m1.astype(jnp.float32) + 0.1 * grad).astype(jnp.bfloat16)
        s_new = (0.95 * m2.astype(jnp.float32) + 0.05 * grad * grad).astype(jnp.bfloat16)
        square = s_new.astype(jnp.float32) * (1.0 / corr_two)
        root = square * lax.rsqrt(square) + EPSILON
        update = f_new.astype(jnp.float32) * (LEARN / corr_one) / root
        t_new = (old.astype(jnp.float32) - update).astype(jnp.bfloat16)
        new_table[rows, :] = jnp.where(kept, t_new, old)
        new_first[rows, :] = jnp.where(kept, f_new, m1)
        new_second[rows, :] = jnp.where(kept, s_new, m2)


def body(hidden, targets, input_ids, input_grads, table, keep, first_moment, second_moment):
    n_pipe, n_vocab = lax.axis_size("pipe"), lax.axis_size("vocab")
    n_x = n_pipe // 2
    here, width = hidden.shape
    vr, half = table.shape
    count = here * 2 * n_pipe * n_vocab
    share = count // 2
    chunks = vr // CHUNK
    bf16, f32 = jnp.bfloat16, jnp.float32
    vmem = pl.BlockSpec(memory_space=pltpu.VMEM)
    dma = pltpu.SemaphoreType.DMA
    dests = n_vocab + n_x - 1
    tokens, grads, dlog, ids, loss = pl.pallas_call(
        functools.partial(head_kernel, n_pipe, n_vocab),
        out_shape=(
            jax.ShapeDtypeStruct((count, half + 128), bf16),
            jax.ShapeDtypeStruct((count, half), bf16),
            jax.ShapeDtypeStruct((2, vr, share), bf16),
            jax.ShapeDtypeStruct((8, count), jnp.int32),
            jax.ShapeDtypeStruct((1, 1), f32),
        ),
        in_specs=[vmem] * 5 + [pl.BlockSpec(memory_space=pl.ANY)],
        out_specs=(vmem,) * 5,
        scratch_shapes=[
            pltpu.VMEM((vr, half), bf16),
            pltpu.VMEM((vr, 1), f32),
            pltpu.VMEM((here, half + 128), bf16),
            pltpu.VMEM((here, half), bf16),
            pltpu.VMEM((8, count), jnp.int32),
            pltpu.VMEM((vr, share), f32),
            pltpu.VMEM((vr, share), f32),
            pltpu.VMEM((vr, share), f32),
            pltpu.VMEM((n_vocab, 8, share), f32),
            pltpu.VMEM((n_x, 8, share), f32),
            pltpu.VMEM((2, 8, share), f32),
            pltpu.VMEM((2, 8, 128), f32),
            dma,
            dma, dma, dma((n_x * n_vocab, dests)), dma((n_pipe * n_vocab,)),
            dma, dma, dma((n_x * n_vocab, dests)), dma((n_pipe * n_vocab,)),
            dma((chunks, n_x)), dma((chunks, n_x)), dma((chunks,)), dma((chunks,)),
            dma((n_vocab,)), dma((n_vocab,)), dma((n_x,)), dma((n_x,)), dma((3,)), dma((3,)),
        ],
        compiler_params=pltpu.CompilerParams(
            collective_id=0, has_side_effects=True, vmem_limit_bytes=VMEM_LIMIT
        ),
        cost_estimate=pl.CostEstimate(
            flops=2 * count * vr * half, bytes_accessed=2 * vr * half, transcendentals=0
        ),
    )(hidden, input_grads, targets[None, :], input_ids[None, :], keep[None, :], table)

    step = math.gcd(half, 256)
    tile = pl.BlockSpec((vr, step), lambda i: (0, i))
    part = pl.BlockSpec((count, step), lambda i: (0, i))
    new_table, new_first, new_second = pl.pallas_call(
        functools.partial(adam_kernel, math.sqrt(width)),
        out_shape=(jax.ShapeDtypeStruct((vr, half), bf16),) * 3,
        grid=(half // step,),
        in_specs=[
            pl.BlockSpec((2, vr, share), lambda i: (0, 0, 0)),
            part, part,
            pl.BlockSpec((8, count), lambda i: (0, 0)),
            pl.BlockSpec((1, vr), lambda i: (0, 0)),
            tile, tile, tile,
        ],
        out_specs=(tile,) * 3,
        scratch_shapes=[pltpu.VMEM((vr, count), bf16), pltpu.VMEM((vr, 1), f32)],
        compiler_params=pltpu.CompilerParams(vmem_limit_bytes=VMEM_LIMIT),
        cost_estimate=pl.CostEstimate(
            flops=4 * count * vr * half, bytes_accessed=12 * vr * half, transcendentals=0
        ),
    )(dlog, tokens, grads, ids, keep[None, :], table, first_moment, second_moment)
    return (new_table, new_first, new_second, loss[0, 0])


def solution(mesh):
    placed = (
        P(("pipe", "dp", "vocab"), None),
        P(("pipe", "dp", "vocab")),
        P(("pipe", "dp", "vocab")),
        P(("pipe", "dp", "vocab"), None),
        P(("pipe", "vocab"), "dp"),
        P(("pipe", "vocab")),
        P(("pipe", "vocab"), "dp"),
        P(("pipe", "vocab"), "dp"),
    )
    return jax.shard_map(
        body,
        mesh=mesh,
        in_specs=placed,
        out_specs=(
            P(("pipe", "vocab"), "dp"),
            P(("pipe", "vocab"), "dp"),
            P(("pipe", "vocab"), "dp"),
            P(),
        ),
        check_vma=False,
    )
```

```python
import functools
import math

import jax
import jax.numpy as jnp
from jax import lax
from jax.experimental import pallas as pl
from jax.experimental.pallas import tpu as pltpu
from jax.sharding import PartitionSpec as P

SOFTCAP = 30.0
LEARN = 0.01
EPSILON = 1e-08
MESH = pl.DeviceIdType.MESH
CHUNK = 256
VMEM_LIMIT = 56 * 2**20


def chunk_rows(c):
    return pl.ds(c * CHUNK, CHUNK)


def row_to_column(row):
    wide = jnp.broadcast_to(row[...].astype(jnp.float32), (8, row.shape[1]))
    return wide.T[:, 0:1]


def id_columns(targets, input_ids):
    count = targets.shape[1]
    square = lax.broadcasted_iota(jnp.int32, (count, count), 0) == lax.broadcasted_iota(
        jnp.int32, (count, count), 1
    )
    lane = lax.broadcasted_iota(jnp.int32, (count, 128), 1)
    result = jnp.zeros((count, 128), jnp.float32)
    rows = [targets[...] >> 8, targets[...] & 255, input_ids[...] >> 8, input_ids[...] & 255]
    for at, row in enumerate(rows):
        column = jnp.sum(
            jnp.where(square, row.astype(jnp.float32), 0.0), axis=1, keepdims=True
        )
        result = jnp.where(lane == at, column, result)
    return result.astype(jnp.bfloat16)


class Gather:
    def __init__(self, place, buf, stage, y_send, y_recv, send, recv):
        self.n_pipe, self.n_vocab, self.pipe, self.dp, self.vocab = place
        self.n_x = self.n_pipe // 2
        self.x, self.core = self.pipe // 2, self.pipe % 2
        self.buf, self.stage = buf, stage
        self.y_send, self.y_recv, self.send, self.recv = y_send, y_recv, send, recv
        self.rows = stage.shape[0]

    def pipe_of(self, k):
        return ((self.x + k) % self.n_x) * 2 + self.core

    def origin(self, k):
        return ((self.x + self.n_x - k) % self.n_x) * 2 + self.core

    def vocab_of(self, k):
        return (self.vocab + k) % self.n_vocab

    def vocab_origin(self, k):
        return (self.vocab + self.n_vocab - k) % self.n_vocab

    def sibling(self):
        return self.pipe + 1 - 2 * self.core

    def block(self, pipe, vocab):
        return (pipe % 2 * self.n_x + pipe // 2) * self.n_vocab + vocab

    def own(self, dp):
        block = self.block(self.pipe, self.vocab)
        return pl.ds(pl.multiple_of((block * 2 + dp) * self.rows, self.rows), self.rows)

    def copy(self, pipe, vocab, slot, dest, device):
        block = self.block(pipe, vocab)
        size = 2 * self.rows
        part = self.buf.at[pl.ds(pl.multiple_of(block * size, size), size)]
        return pltpu.make_async_remote_copy(
            src_ref=part, dst_ref=part,
            send_sem=self.send.at[slot, dest], recv_sem=self.recv.at[block],
            device_id=device, device_id_type=MESH,
        )

    def start(self, pipe, vocab, slot, dest, device):
        copy = self.copy(pipe, vocab, slot, dest, device)
        copy.start()

    def pair_copy(self):
        return pltpu.make_async_remote_copy(
            src_ref=self.stage, dst_ref=self.buf.at[self.own(self.dp)],
            send_sem=self.y_send, recv_sem=self.y_recv,
            device_id={"dp": 1 - self.dp}, device_id_type=MESH,
        )

    def pair(self):
        copy = self.pair_copy()
        copy.start()
        self.first = copy

    def to_x(self, pipe, vocab, slot):
        for k in range(1, self.n_x):
            self.start(pipe, vocab, slot, 1 + k, {"pipe": self.pipe_of(k)})

    def to_core(self, pipe, vocab, slot):
        self.start(pipe, vocab, slot, self.n_x + 1, {"pipe": self.sibling()})

    def arrived(self, pipe, vocab):
        self.copy(pipe, vocab, 0, 0, {"pipe": self.sibling()}).wait_recv()

    def spread(self):
        self.first.wait_recv()
        self.to_x(self.pipe, self.vocab, 0)
        self.to_right(self.vocab, 0)
        self.to_left(self.vocab, 0)
        self.to_core(self.pipe, self.vocab, 0)

    def to_right(self, vocab, slot):
        @pl.when(self.vocab < self.n_vocab - 1)
        def _():
            self.start(self.pipe, vocab, slot, 0, {"vocab": self.vocab + 1})

    def to_left(self, vocab, slot):
        @pl.when(self.vocab > 0)
        def _():
            self.start(self.pipe, vocab, slot, 1, {"vocab": self.vocab - 1})

    def relay_near(self):
        for k in range(1, self.n_vocab):

            @pl.when(self.vocab >= k)
            def _():
                source = self.vocab - k
                self.arrived(self.pipe, source)
                self.to_right(source, k)
                self.to_x(self.pipe, source, k)
                self.to_core(self.pipe, source, k)

            @pl.when(self.vocab + k < self.n_vocab)
            def _():
                source, slot = self.vocab + k, self.n_vocab - k
                self.arrived(self.pipe, source)
                self.to_left(source, slot)
                self.to_x(self.pipe, source, slot)
                self.to_core(self.pipe, source, slot)

    def relay_far(self, j):
        for k in range(self.n_vocab):
            pipe, source = self.origin(j), self.vocab_origin(k)
            self.arrived(pipe, source)
            self.to_core(pipe, source, j * self.n_vocab + k)

    def finish(self, j):
        for k in range(self.n_vocab):
            pipe = self.origin(j) + 1 - 2 * self.core
            self.arrived(pipe, self.vocab_origin(k))

    def sent(self):
        self.first.wait_send()
        for k in range(self.n_vocab):

            @pl.when((self.vocab >= k) & (self.vocab < self.n_vocab - 1))
            def _():
                self.sent_one(self.pipe, self.vocab - k, k, 0)

            @pl.when((self.vocab + k < self.n_vocab) & (self.vocab > 0))
            def _():
                self.sent_one(self.pipe, self.vocab + k, (self.n_vocab - k) % self.n_vocab, 1)

            source = self.vocab_origin(k)
            for j in range(1, self.n_x):
                self.sent_one(self.pipe, source, k, 1 + j)
            for j in range(self.n_x):
                self.sent_one(self.origin(j), source, j * self.n_vocab + k, self.n_x + 1)

    def sent_one(self, pipe, vocab, slot, dest):
        self.copy(pipe, vocab, slot, dest, {"pipe": self.sibling()}).wait_send()


def head_kernel(
    n_pipe, n_vocab, hid, grd, aims, reads, keep_row, table_hbm,
    hbuf, gbuf, dlog, ids, loss,
    table, keep, hstage, gstage, goals, outgoing, incoming, logits, v_sum, x_sum, c_sum, losses,
    table_sem, hy_send, hy_recv, h_send, h_recv, gy_send, gy_recv, g_send, g_recv,
    l_send, l_recv, d_send, d_recv, vs_send, vs_recv, xs_send, xs_recv, one_send, one_recv,
):
    pipe, dp, vocab = lax.axis_index("pipe"), lax.axis_index("dp"), lax.axis_index("vocab")
    place = (n_pipe, n_vocab, pipe, dp, vocab)
    other = 1 - dp
    vr, half = table.shape
    share = outgoing.shape[1]
    chunks = vr // CHUNK
    row_start = (pipe * n_vocab + vocab) * vr

    load = pltpu.make_async_copy(table_hbm, table, table_sem)
    load.start()
    h = Gather(place, hbuf, hstage, hy_send, hy_recv, h_send, h_recv)
    g = Gather(place, gbuf, gstage, gy_send, gy_recv, g_send, g_recv)

    barrier = pltpu.get_barrier_semaphore()
    peers = [{"dp": other}, {"pipe": h.sibling()}]
    peers += [{"vocab": h.vocab_of(k)} for k in range(1, n_vocab)]
    peers += [{"pipe": h.pipe_of(k)} for k in range(1, h.n_x)]
    for peer in peers:
        pl.semaphore_signal(barrier, inc=1, device_id=peer, device_id_type=MESH)

    mine = pl.ds(pl.multiple_of(dp * half, 128), half)
    theirs = pl.ds(pl.multiple_of(other * half, 128), half)
    hstage[:, :half] = hid[:, theirs]
    meta = id_columns(aims, reads)
    hstage[:, half:] = meta
    hbuf[h.own(dp), :half] = hid[:, mine]
    hbuf[h.own(dp), half:] = meta
    gstage[...] = grd[:, theirs]
    gbuf[g.own(dp), :] = grd[:, mine]
    pl.semaphore_wait(barrier, len(peers))

    h.pair()
    h.spread()
    g.pair()
    keep[...] = row_to_column(keep_row)
    h.relay_near()
    load.wait()

    group = share // h.n_x

    def partial(c, which, x):
        start = pl.multiple_of(which * share + x * group, group)
        return lax.dot_general(
            table[chunk_rows(c), :], hbuf[pl.ds(start, group), :half],
            (((1,), (1,)), ((), ())), preferred_element_type=jnp.float32,
        )

    def exchange(source, dest, send_sem, recv_sem, device):
        return pltpu.make_async_remote_copy(
            src_ref=source, dst_ref=dest, send_sem=send_sem, recv_sem=recv_sem,
            device_id=device, device_id_type=MESH,
        )

    logit_copies = []
    for j in range(h.n_x):
        if j:
            h.relay_far(j)
        h.finish(j)
        if j == h.n_x - 1:
            g.spread()
        x = h.origin(j) // 2
        lanes = pl.ds(pl.multiple_of(x * group, group), group)
        for c in range(chunks):
            rows = chunk_rows(c)
            outgoing[rows, lanes] = partial(c, other, x)
            copy = exchange(
                outgoing.at[rows, lanes], incoming.at[rows, lanes],
                l_send.at[c, x], l_recv.at[c, x], {"dp": other},
            )
            copy.start()
            logit_copies.append(copy)
        for c in range(chunks):
            logits[chunk_rows(c), lanes] = partial(c, dp, x)
    spots = hbuf[:, half:].astype(jnp.float32).T
    goals[...] = jnp.broadcast_to(
        (spots[0:1] * 256.0 + spots[1:2]).astype(jnp.int32) - row_start, goals.shape
    )
    ids[...] = jnp.broadcast_to(
        (spots[2:3] * 256.0 + spots[3:4]).astype(jnp.int32) - row_start, ids.shape
    )
    g.relay_near()
    for j in range(1, g.n_x):
        g.relay_far(j)

    goal = goals[0:1, pl.ds(pl.multiple_of(dp * share, share), share)]
    row_iota = lax.broadcasted_iota(jnp.int32, (CHUNK, share), 0)
    total = jnp.zeros((1, share), jnp.float32)
    target = jnp.zeros((1, share), jnp.float32)
    for c in range(chunks):
        rows = chunk_rows(c)
        for x in range(h.n_x):
            lanes = pl.ds(x * group, group)
            exchange(
                outgoing.at[rows, lanes], incoming.at[rows, lanes],
                l_send.at[c, x], l_recv.at[c, x], {"dp": other},
            ).wait_recv()
        unit = jnp.tanh((logits[rows, :] + incoming[rows, :]) * (1.0 / SOFTCAP))
        capped = SOFTCAP * unit
        weights = jnp.exp(capped) * keep[rows, :]
        hit = row_iota == goal - c * CHUNK
        total += jnp.sum(weights, axis=0, keepdims=True)
        target += jnp.sum(jnp.where(hit, capped, 0.0), axis=0, keepdims=True)
        logits[rows, :] = unit
        incoming[rows, :] = weights

    small = []

    def summed(slots, index, count, offsets, peer, send, recv):
        for k in offsets:
            copy = exchange(slots.at[index], slots.at[index], send.at[k], recv.at[index], peer(k))
            copy.start()
            small.append(copy)
        for k in offsets:
            source = (index + count - k) % count
            exchange(
                slots.at[source], slots.at[source], send.at[k], recv.at[source], peer(k)
            ).wait_recv()
        value = slots[0]
        for k in range(1, count):
            value = value + slots[k]
        return value

    v_sum[vocab, 0:1] = total
    v_sum[vocab, 1:2] = target
    v_sum[vocab, 2:8] = jnp.zeros((6, share), jnp.float32)
    x_sum[h.x] = summed(
        v_sum, vocab, n_vocab, range(1, n_vocab),
        lambda k: {"vocab": h.vocab_of(k)}, vs_send, vs_recv,
    )
    c_sum[h.core] = summed(
        x_sum, h.x, h.n_x, range(1, h.n_x),
        lambda k: {"pipe": h.pipe_of(k)}, xs_send, xs_recv,
    )
    sums = summed(
        c_sum, h.core, 2, range(1, 2),
        lambda k: {"pipe": h.sibling()}, one_send, one_recv,
    )
    total, target = sums[0:1], sums[1:2]
    inverse = 1.0 / total
    dlogit_copies = []
    for c in range(chunks):
        rows = chunk_rows(c)
        unit = logits[rows, :]
        hit = row_iota == goal - c * CHUNK
        slope = 1.0 - unit * unit
        value = (incoming[rows, :] * inverse - jnp.where(hit, 1.0, 0.0)) * slope
        dlog[dp, rows, :] = value.astype(jnp.bfloat16)
        part = dlog.at[dp, rows]
        copy = exchange(part, part, d_send.at[c], d_recv.at[c], {"dp": other})
        copy.start()
        dlogit_copies.append(copy)
    piece = jnp.sum(jnp.log(total) - target, axis=1, keepdims=True)
    losses[dp] = jnp.broadcast_to(piece, losses.shape[1:])
    part = losses.at[dp]
    copy = exchange(part, part, one_send.at[2], one_recv.at[2], {"dp": other})
    copy.start()
    for j in range(g.n_x):
        g.finish(j)
    copy.wait()
    loss[...] = losses[0, 0:1, 0:1] + losses[1, 0:1, 0:1]
    for copy in dlogit_copies:
        copy.wait()
    for copy in logit_copies + small:
        copy.wait_send()
    h.sent()
    g.sent()


def adam_kernel(scale, dlog, tokens, grads, ids, keep, table, first, second, *rest):
    new_table, new_first, new_second, selector, kept_column = rest
    share = dlog.shape[2]

    @pl.when(pl.program_id(0) == 0)
    def _():
        row_iota = lax.broadcasted_iota(jnp.int32, selector.shape, 0)
        hit = ids[0:1, :] == row_iota
        selector[...] = jnp.where(hit, 1.0, 0.0).astype(jnp.bfloat16)
        kept_column[...] = row_to_column(keep)

    corr_one = 1.0 - 0.9**10
    corr_two = 1.0 - 0.95**10
    for c in range(table.shape[0] // CHUNK):
        rows = chunk_rows(c)
        kept = kept_column[rows, :] > 0.0
        grad = scale * jnp.dot(
            selector[rows, :], grads[...], preferred_element_type=jnp.float32
        )
        for j in range(2):
            grad += jnp.dot(
                dlog[j, rows, :], tokens[j * share:(j + 1) * share, :],
                preferred_element_type=jnp.float32,
            )
        m1, m2, old = first[rows, :], second[rows, :], table[rows, :]
        f_new = (0.9 * m1.astype(jnp.float32) + 0.1 * grad).astype(jnp.bfloat16)
        s_new = (0.95 * m2.astype(jnp.float32) + 0.05 * grad * grad).astype(jnp.bfloat16)
        square = s_new.astype(jnp.float32) * (1.0 / corr_two)
        root = square * lax.rsqrt(square) + EPSILON
        update = f_new.astype(jnp.float32) * (LEARN / corr_one) / root
        t_new = (old.astype(jnp.float32) - update).astype(jnp.bfloat16)
        new_table[rows, :] = jnp.where(kept, t_new, old)
        new_first[rows, :] = jnp.where(kept, f_new, m1)
        new_second[rows, :] = jnp.where(kept, s_new, m2)


def body(hidden, targets, input_ids, input_grads, table, keep, first_moment, second_moment):
    n_pipe, n_vocab = lax.axis_size("pipe"), lax.axis_size("vocab")
    n_x = n_pipe // 2
    here, width = hidden.shape
    vr, half = table.shape
    count = here * 2 * n_pipe * n_vocab
    share = count // 2
    chunks = vr // CHUNK
    bf16, f32 = jnp.bfloat16, jnp.float32
    vmem = pl.BlockSpec(memory_space=pltpu.VMEM)
    dma = pltpu.SemaphoreType.DMA
    dests = n_x + 2
    tokens, grads, dlog, ids, loss = pl.pallas_call(
        functools.partial(head_kernel, n_pipe, n_vocab),
        out_shape=(
            jax.ShapeDtypeStruct((count, half + 128), bf16),
            jax.ShapeDtypeStruct((count, half), bf16),
            jax.ShapeDtypeStruct((2, vr, share), bf16),
            jax.ShapeDtypeStruct((8, count), jnp.int32),
            jax.ShapeDtypeStruct((1, 1), f32),
        ),
        in_specs=[vmem] * 5 + [pl.BlockSpec(memory_space=pl.ANY)],
        out_specs=(vmem,) * 5,
        scratch_shapes=[
            pltpu.VMEM((vr, half), bf16),
            pltpu.VMEM((vr, 1), f32),
            pltpu.VMEM((here, half + 128), bf16),
            pltpu.VMEM((here, half), bf16),
            pltpu.VMEM((8, count), jnp.int32),
            pltpu.VMEM((vr, share), f32),
            pltpu.VMEM((vr, share), f32),
            pltpu.VMEM((vr, share), f32),
            pltpu.VMEM((n_vocab, 8, share), f32),
            pltpu.VMEM((n_x, 8, share), f32),
            pltpu.VMEM((2, 8, share), f32),
            pltpu.VMEM((2, 8, 128), f32),
            dma,
            dma, dma, dma((n_x * n_vocab, dests)), dma((n_pipe * n_vocab,)),
            dma, dma, dma((n_x * n_vocab, dests)), dma((n_pipe * n_vocab,)),
            dma((chunks, n_x)), dma((chunks, n_x)), dma((chunks,)), dma((chunks,)),
            dma((n_vocab,)), dma((n_vocab,)), dma((n_x,)), dma((n_x,)), dma((3,)), dma((3,)),
        ],
        compiler_params=pltpu.CompilerParams(
            collective_id=0, has_side_effects=True, vmem_limit_bytes=VMEM_LIMIT
        ),
        cost_estimate=pl.CostEstimate(
            flops=2 * count * vr * half, bytes_accessed=2 * vr * half, transcendentals=0
        ),
    )(hidden, input_grads, targets[None, :], input_ids[None, :], keep[None, :], table)

    step = math.gcd(half, 256)
    tile = pl.BlockSpec((vr, step), lambda i: (0, i))
    part = pl.BlockSpec((count, step), lambda i: (0, i))
    new_table, new_first, new_second = pl.pallas_call(
        functools.partial(adam_kernel, math.sqrt(width)),
        out_shape=(jax.ShapeDtypeStruct((vr, half), bf16),) * 3,
        grid=(half // step,),
        in_specs=[
            pl.BlockSpec((2, vr, share), lambda i: (0, 0, 0)),
            part, part,
            pl.BlockSpec((8, count), lambda i: (0, 0)),
            pl.BlockSpec((1, vr), lambda i: (0, 0)),
            tile, tile, tile,
        ],
        out_specs=(tile,) * 3,
        scratch_shapes=[pltpu.VMEM((vr, count), bf16), pltpu.VMEM((vr, 1), f32)],
        compiler_params=pltpu.CompilerParams(vmem_limit_bytes=VMEM_LIMIT),
        cost_estimate=pl.CostEstimate(
            flops=4 * count * vr * half, bytes_accessed=12 * vr * half, transcendentals=0
        ),
    )(dlog, tokens, grads, ids, keep[None, :], table, first_moment, second_moment)
    return (new_table, new_first, new_second, loss[0, 0])


def solution(mesh):
    placed = (
        P(("pipe", "dp", "vocab"), None),
        P(("pipe", "dp", "vocab")),
        P(("pipe", "dp", "vocab")),
        P(("pipe", "dp", "vocab"), None),
        P(("pipe", "vocab"), "dp"),
        P(("pipe", "vocab")),
        P(("pipe", "vocab"), "dp"),
        P(("pipe", "vocab"), "dp"),
    )
    return jax.shard_map(
        body,
        mesh=mesh,
        in_specs=placed,
        out_specs=(
            P(("pipe", "vocab"), "dp"),
            P(("pipe", "vocab"), "dp"),
            P(("pipe", "vocab"), "dp"),
            P(),
        ),
        check_vma=False,
    )
```

```python
import functools
import math

import jax
import jax.numpy as jnp
from jax import lax
from jax.experimental import pallas as pl
from jax.experimental.pallas import tpu as pltpu
from jax.sharding import PartitionSpec as P

SOFTCAP = 30.0
LEARN = 0.01
EPSILON = 1e-08
MESH = pl.DeviceIdType.MESH
CHUNK = 256
VMEM_LIMIT = 56 * 2**20


def chunk_rows(c):
    return pl.ds(c * CHUNK, CHUNK)


def row_to_column(row):
    wide = jnp.broadcast_to(row[...].astype(jnp.float32), (8, row.shape[1]))
    return wide.T[:, 0:1]


def id_columns(targets, input_ids):
    count = targets.shape[1]
    square = lax.broadcasted_iota(jnp.int32, (count, count), 0) == lax.broadcasted_iota(
        jnp.int32, (count, count), 1
    )
    lane = lax.broadcasted_iota(jnp.int32, (count, 128), 1)
    result = jnp.zeros((count, 128), jnp.float32)
    rows = [targets[...] >> 8, targets[...] & 255, input_ids[...] >> 8, input_ids[...] & 255]
    for at, row in enumerate(rows):
        column = jnp.sum(
            jnp.where(square, row.astype(jnp.float32), 0.0), axis=1, keepdims=True
        )
        result = jnp.where(lane == at, column, result)
    return result.astype(jnp.bfloat16)


class Gather:
    def __init__(self, place, buf, stage, y_send, y_recv, send, recv):
        self.n_pipe, self.n_vocab, self.pipe, self.dp, self.vocab = place
        self.n_x = self.n_pipe // 2
        self.x, self.core = self.pipe // 2, self.pipe % 2
        self.buf, self.stage = buf, stage
        self.y_send, self.y_recv, self.send, self.recv = y_send, y_recv, send, recv
        self.rows = stage.shape[0]

    def pipe_of(self, k):
        return ((self.x + k) % self.n_x) * 2 + self.core

    def origin(self, k):
        return ((self.x + self.n_x - k) % self.n_x) * 2 + self.core

    def vocab_of(self, k):
        return (self.vocab + k) % self.n_vocab

    def vocab_origin(self, k):
        return (self.vocab + self.n_vocab - k) % self.n_vocab

    def sibling(self):
        return self.pipe + 1 - 2 * self.core

    def block(self, pipe, vocab):
        return (pipe % 2 * self.n_x + pipe // 2) * self.n_vocab + vocab

    def own(self, dp):
        block = self.block(self.pipe, self.vocab)
        return pl.ds(pl.multiple_of((block * 2 + dp) * self.rows, self.rows), self.rows)

    def copy(self, pipe, vocab, slot, dest, device):
        block = self.block(pipe, vocab)
        size = 2 * self.rows
        part = self.buf.at[pl.ds(pl.multiple_of(block * size, size), size)]
        return pltpu.make_async_remote_copy(
            src_ref=part, dst_ref=part,
            send_sem=self.send.at[slot, dest], recv_sem=self.recv.at[block],
            device_id=device, device_id_type=MESH,
        )

    def start(self, pipe, vocab, slot, dest, device):
        copy = self.copy(pipe, vocab, slot, dest, device)
        copy.start()

    def pair_copy(self):
        return pltpu.make_async_remote_copy(
            src_ref=self.stage, dst_ref=self.buf.at[self.own(self.dp)],
            send_sem=self.y_send, recv_sem=self.y_recv,
            device_id={"dp": 1 - self.dp}, device_id_type=MESH,
        )

    def pair(self):
        copy = self.pair_copy()
        copy.start()
        self.first = copy

    def to_x(self, pipe, vocab, slot):
        for k in range(1, self.n_x):
            self.start(pipe, vocab, slot, 1 + k, {"pipe": self.pipe_of(k)})

    def to_core(self, pipe, vocab, slot):
        self.start(pipe, vocab, slot, self.n_x + 1, {"pipe": self.sibling()})

    def arrived(self, pipe, vocab):
        self.copy(pipe, vocab, 0, 0, {"pipe": self.sibling()}).wait_recv()

    def spread(self):
        self.first.wait_recv()
        self.to_x(self.pipe, self.vocab, 0)
        self.to_right(self.vocab, 0)
        self.to_left(self.vocab, 0)
        self.to_core(self.pipe, self.vocab, 0)

    def to_right(self, vocab, slot):
        @pl.when(self.vocab < self.n_vocab - 1)
        def _():
            self.start(self.pipe, vocab, slot, 0, {"vocab": self.vocab + 1})

    def to_left(self, vocab, slot):
        @pl.when(self.vocab > 0)
        def _():
            self.start(self.pipe, vocab, slot, 1, {"vocab": self.vocab - 1})

    def relay_near(self):
        for k in range(1, self.n_vocab):

            @pl.when(self.vocab >= k)
            def _():
                source = self.vocab - k
                self.arrived(self.pipe, source)
                self.to_right(source, k)
                self.to_x(self.pipe, source, k)
                self.to_core(self.pipe, source, k)

            @pl.when(self.vocab + k < self.n_vocab)
            def _():
                source, slot = self.vocab + k, self.n_vocab - k
                self.arrived(self.pipe, source)
                self.to_left(source, slot)
                self.to_x(self.pipe, source, slot)
                self.to_core(self.pipe, source, slot)

    def relay_far(self, j):
        for k in range(self.n_vocab):
            pipe, source = self.origin(j), self.vocab_origin(k)
            self.arrived(pipe, source)
            self.to_core(pipe, source, j * self.n_vocab + k)

    def finish(self, j):
        for k in range(self.n_vocab):
            pipe = self.origin(j) + 1 - 2 * self.core
            self.arrived(pipe, self.vocab_origin(k))

    def sent(self):
        self.first.wait_send()
        for k in range(self.n_vocab):

            @pl.when((self.vocab >= k) & (self.vocab < self.n_vocab - 1))
            def _():
                self.sent_one(self.pipe, self.vocab - k, k, 0)

            @pl.when((self.vocab + k < self.n_vocab) & (self.vocab > 0))
            def _():
                self.sent_one(self.pipe, self.vocab + k, (self.n_vocab - k) % self.n_vocab, 1)

            source = self.vocab_origin(k)
            for j in range(1, self.n_x):
                self.sent_one(self.pipe, source, k, 1 + j)
            for j in range(self.n_x):
                self.sent_one(self.origin(j), source, j * self.n_vocab + k, self.n_x + 1)

    def sent_one(self, pipe, vocab, slot, dest):
        self.copy(pipe, vocab, slot, dest, {"pipe": self.sibling()}).wait_send()


def head_kernel(
    n_pipe, n_vocab, hid, grd, aims, reads, keep_row, table_hbm,
    hbuf, gbuf, dlog, ids, loss,
    table, keep, hstage, gstage, goals, outgoing, incoming, logits, v_sum, x_sum, c_sum, losses,
    table_sem, hy_send, hy_recv, h_send, h_recv, gy_send, gy_recv, g_send, g_recv,
    l_send, l_recv, d_send, d_recv, vs_send, vs_recv, xs_send, xs_recv, one_send, one_recv,
):
    pipe, dp, vocab = lax.axis_index("pipe"), lax.axis_index("dp"), lax.axis_index("vocab")
    place = (n_pipe, n_vocab, pipe, dp, vocab)
    other = 1 - dp
    vr, half = table.shape
    share = outgoing.shape[1]
    chunks = vr // CHUNK
    row_start = (pipe * n_vocab + vocab) * vr

    load = pltpu.make_async_copy(table_hbm, table, table_sem)
    load.start()
    h = Gather(place, hbuf, hstage, hy_send, hy_recv, h_send, h_recv)
    g = Gather(place, gbuf, gstage, gy_send, gy_recv, g_send, g_recv)

    barrier = pltpu.get_barrier_semaphore()
    peers = [{"dp": other}, {"pipe": h.sibling()}]
    peers += [{"vocab": h.vocab_of(k)} for k in range(1, n_vocab)]
    peers += [{"pipe": h.pipe_of(k)} for k in range(1, h.n_x)]
    for peer in peers:
        pl.semaphore_signal(barrier, inc=1, device_id=peer, device_id_type=MESH)

    mine = pl.ds(pl.multiple_of(dp * half, 128), half)
    theirs = pl.ds(pl.multiple_of(other * half, 128), half)
    hstage[:, :half] = hid[:, theirs]
    meta = id_columns(aims, reads)
    hstage[:, half:] = meta
    hbuf[h.own(dp), :half] = hid[:, mine]
    hbuf[h.own(dp), half:] = meta
    gstage[...] = grd[:, theirs]
    gbuf[g.own(dp), :] = grd[:, mine]
    pl.semaphore_wait(barrier, len(peers))

    h.pair()
    h.spread()
    g.pair()
    keep[...] = row_to_column(keep_row)
    h.relay_near()
    load.wait()

    group = share // h.n_x

    def partial(c, which, x):
        start = pl.multiple_of(which * share + x * group, group)
        return lax.dot_general(
            table[chunk_rows(c), :], hbuf[pl.ds(start, group), :half],
            (((1,), (1,)), ((), ())), preferred_element_type=jnp.float32,
        )

    def exchange(source, dest, send_sem, recv_sem, device):
        return pltpu.make_async_remote_copy(
            src_ref=source, dst_ref=dest, send_sem=send_sem, recv_sem=recv_sem,
            device_id=device, device_id_type=MESH,
        )

    logit_copies = []
    for j in range(h.n_x):
        if j:
            h.relay_far(j)
        if j == h.n_x - 1:
            g.spread()
        h.finish(j)
        x = h.origin(j) // 2
        lanes = pl.ds(pl.multiple_of(x * group, group), group)
        for c in range(chunks):
            rows = chunk_rows(c)
            outgoing[rows, lanes] = partial(c, other, x)
            copy = exchange(
                outgoing.at[rows, lanes], incoming.at[rows, lanes],
                l_send.at[c, x], l_recv.at[c, x], {"dp": other},
            )
            copy.start()
            logit_copies.append(copy)
        for c in range(chunks):
            logits[chunk_rows(c), lanes] = partial(c, dp, x)
    spots = hbuf[:, half:].astype(jnp.float32).T
    goals[...] = jnp.broadcast_to(
        (spots[0:1] * 256.0 + spots[1:2]).astype(jnp.int32) - row_start, goals.shape
    )
    ids[...] = jnp.broadcast_to(
        (spots[2:3] * 256.0 + spots[3:4]).astype(jnp.int32) - row_start, ids.shape
    )
    g.relay_near()
    for j in range(1, g.n_x):
        g.relay_far(j)

    goal = goals[0:1, pl.ds(pl.multiple_of(dp * share, share), share)]
    row_iota = lax.broadcasted_iota(jnp.int32, (CHUNK, share), 0)
    total = jnp.zeros((1, share), jnp.float32)
    target = jnp.zeros((1, share), jnp.float32)
    for c in range(chunks):
        rows = chunk_rows(c)
        for x in range(h.n_x):
            lanes = pl.ds(x * group, group)
            exchange(
                outgoing.at[rows, lanes], incoming.at[rows, lanes],
                l_send.at[c, x], l_recv.at[c, x], {"dp": other},
            ).wait_recv()
        unit = jnp.tanh((logits[rows, :] + incoming[rows, :]) * (1.0 / SOFTCAP))
        capped = SOFTCAP * unit
        weights = jnp.exp(capped) * keep[rows, :]
        hit = row_iota == goal - c * CHUNK
        total += jnp.sum(weights, axis=0, keepdims=True)
        target += jnp.sum(jnp.where(hit, capped, 0.0), axis=0, keepdims=True)
        logits[rows, :] = unit
        incoming[rows, :] = weights

    small = []

    def summed(slots, index, count, offsets, peer, send, recv):
        for k in offsets:
            copy = exchange(slots.at[index], slots.at[index], send.at[k], recv.at[index], peer(k))
            copy.start()
            small.append(copy)
        for k in offsets:
            source = (index + count - k) % count
            exchange(
                slots.at[source], slots.at[source], send.at[k], recv.at[source], peer(k)
            ).wait_recv()
        value = slots[0]
        for k in range(1, count):
            value = value + slots[k]
        return value

    v_sum[vocab, 0:1] = total
    v_sum[vocab, 1:2] = target
    v_sum[vocab, 2:8] = jnp.zeros((6, share), jnp.float32)
    x_sum[h.x] = summed(
        v_sum, vocab, n_vocab, range(1, n_vocab),
        lambda k: {"vocab": h.vocab_of(k)}, vs_send, vs_recv,
    )
    c_sum[h.core] = summed(
        x_sum, h.x, h.n_x, range(1, h.n_x),
        lambda k: {"pipe": h.pipe_of(k)}, xs_send, xs_recv,
    )
    sums = summed(
        c_sum, h.core, 2, range(1, 2),
        lambda k: {"pipe": h.sibling()}, one_send, one_recv,
    )
    total, target = sums[0:1], sums[1:2]
    inverse = 1.0 / total
    dlogit_copies = []
    for c in range(chunks):
        rows = chunk_rows(c)
        unit = logits[rows, :]
        hit = row_iota == goal - c * CHUNK
        slope = 1.0 - unit * unit
        value = (incoming[rows, :] * inverse - jnp.where(hit, 1.0, 0.0)) * slope
        dlog[dp, rows, :] = value.astype(jnp.bfloat16)
        part = dlog.at[dp, rows]
        copy = exchange(part, part, d_send.at[c], d_recv.at[c], {"dp": other})
        copy.start()
        dlogit_copies.append(copy)
    piece = jnp.sum(jnp.log(total) - target, axis=1, keepdims=True)
    losses[dp] = jnp.broadcast_to(piece, losses.shape[1:])
    part = losses.at[dp]
    copy = exchange(part, part, one_send.at[2], one_recv.at[2], {"dp": other})
    copy.start()
    for j in range(g.n_x):
        g.finish(j)
    copy.wait()
    loss[...] = losses[0, 0:1, 0:1] + losses[1, 0:1, 0:1]
    for copy in dlogit_copies:
        copy.wait()
    for copy in logit_copies + small:
        copy.wait_send()
    h.sent()
    g.sent()


def adam_kernel(scale, dlog, tokens, grads, ids, keep, table, first, second, *rest):
    new_table, new_first, new_second, selector, kept_column = rest
    share = dlog.shape[2]

    @pl.when(pl.program_id(0) == 0)
    def _():
        row_iota = lax.broadcasted_iota(jnp.int32, selector.shape, 0)
        hit = ids[0:1, :] == row_iota
        selector[...] = jnp.where(hit, 1.0, 0.0).astype(jnp.bfloat16)
        kept_column[...] = row_to_column(keep)

    corr_one = 1.0 - 0.9**10
    corr_two = 1.0 - 0.95**10
    size = CHUNK // 2
    for c in range(table.shape[0] // size):
        rows = pl.ds(c * size, size)
        kept = kept_column[rows, :] > 0.0
        grad = scale * jnp.dot(
            selector[rows, :], grads[...], preferred_element_type=jnp.float32
        )
        for j in range(2):
            grad += jnp.dot(
                dlog[j, rows, :], tokens[j * share:(j + 1) * share, :],
                preferred_element_type=jnp.float32,
            )
        m1, m2, old = first[rows, :], second[rows, :], table[rows, :]
        f_new = (0.9 * m1.astype(jnp.float32) + 0.1 * grad).astype(jnp.bfloat16)
        s_new = (0.95 * m2.astype(jnp.float32) + 0.05 * grad * grad).astype(jnp.bfloat16)
        square = s_new.astype(jnp.float32) * (1.0 / corr_two)
        root = square * lax.rsqrt(square) + EPSILON
        update = f_new.astype(jnp.float32) * (LEARN / corr_one) / root
        t_new = (old.astype(jnp.float32) - update).astype(jnp.bfloat16)
        new_table[rows, :] = jnp.where(kept, t_new, old)
        new_first[rows, :] = jnp.where(kept, f_new, m1)
        new_second[rows, :] = jnp.where(kept, s_new, m2)


def body(hidden, targets, input_ids, input_grads, table, keep, first_moment, second_moment):
    n_pipe, n_vocab = lax.axis_size("pipe"), lax.axis_size("vocab")
    n_x = n_pipe // 2
    here, width = hidden.shape
    vr, half = table.shape
    count = here * 2 * n_pipe * n_vocab
    share = count // 2
    chunks = vr // CHUNK
    bf16, f32 = jnp.bfloat16, jnp.float32
    vmem = pl.BlockSpec(memory_space=pltpu.VMEM)
    dma = pltpu.SemaphoreType.DMA
    dests = n_x + 2
    tokens, grads, dlog, ids, loss = pl.pallas_call(
        functools.partial(head_kernel, n_pipe, n_vocab),
        out_shape=(
            jax.ShapeDtypeStruct((count, half + 128), bf16),
            jax.ShapeDtypeStruct((count, half), bf16),
            jax.ShapeDtypeStruct((2, vr, share), bf16),
            jax.ShapeDtypeStruct((8, count), jnp.int32),
            jax.ShapeDtypeStruct((1, 1), f32),
        ),
        in_specs=[vmem] * 5 + [pl.BlockSpec(memory_space=pl.ANY)],
        out_specs=(vmem,) * 5,
        scratch_shapes=[
            pltpu.VMEM((vr, half), bf16),
            pltpu.VMEM((vr, 1), f32),
            pltpu.VMEM((here, half + 128), bf16),
            pltpu.VMEM((here, half), bf16),
            pltpu.VMEM((8, count), jnp.int32),
            pltpu.VMEM((vr, share), f32),
            pltpu.VMEM((vr, share), f32),
            pltpu.VMEM((vr, share), f32),
            pltpu.VMEM((n_vocab, 8, share), f32),
            pltpu.VMEM((n_x, 8, share), f32),
            pltpu.VMEM((2, 8, share), f32),
            pltpu.VMEM((2, 8, 128), f32),
            dma,
            dma, dma, dma((n_x * n_vocab, dests)), dma((n_pipe * n_vocab,)),
            dma, dma, dma((n_x * n_vocab, dests)), dma((n_pipe * n_vocab,)),
            dma((chunks, n_x)), dma((chunks, n_x)), dma((chunks,)), dma((chunks,)),
            dma((n_vocab,)), dma((n_vocab,)), dma((n_x,)), dma((n_x,)), dma((3,)), dma((3,)),
        ],
        compiler_params=pltpu.CompilerParams(
            collective_id=0, has_side_effects=True, vmem_limit_bytes=VMEM_LIMIT
        ),
        cost_estimate=pl.CostEstimate(
            flops=2 * count * vr * half, bytes_accessed=2 * vr * half, transcendentals=0
        ),
    )(hidden, input_grads, targets[None, :], input_ids[None, :], keep[None, :], table)

    step = math.gcd(half, 256)
    tile = pl.BlockSpec((vr, step), lambda i: (0, i))
    part = pl.BlockSpec((count, step), lambda i: (0, i))
    new_table, new_first, new_second = pl.pallas_call(
        functools.partial(adam_kernel, math.sqrt(width)),
        out_shape=(jax.ShapeDtypeStruct((vr, half), bf16),) * 3,
        grid=(half // step,),
        in_specs=[
            pl.BlockSpec((2, vr, share), lambda i: (0, 0, 0)),
            part, part,
            pl.BlockSpec((8, count), lambda i: (0, 0)),
            pl.BlockSpec((1, vr), lambda i: (0, 0)),
            tile, tile, tile,
        ],
        out_specs=(tile,) * 3,
        scratch_shapes=[pltpu.VMEM((vr, count), bf16), pltpu.VMEM((vr, 1), f32)],
        compiler_params=pltpu.CompilerParams(vmem_limit_bytes=VMEM_LIMIT),
        cost_estimate=pl.CostEstimate(
            flops=4 * count * vr * half, bytes_accessed=12 * vr * half, transcendentals=0
        ),
    )(dlog, tokens, grads, ids, keep[None, :], table, first_moment, second_moment)
    return (new_table, new_first, new_second, loss[0, 0])


def solution(mesh):
    placed = (
        P(("pipe", "dp", "vocab"), None),
        P(("pipe", "dp", "vocab")),
        P(("pipe", "dp", "vocab")),
        P(("pipe", "dp", "vocab"), None),
        P(("pipe", "vocab"), "dp"),
        P(("pipe", "vocab")),
        P(("pipe", "vocab"), "dp"),
        P(("pipe", "vocab"), "dp"),
    )
    return jax.shard_map(
        body,
        mesh=mesh,
        in_specs=placed,
        out_specs=(
            P(("pipe", "vocab"), "dp"),
            P(("pipe", "vocab"), "dp"),
            P(("pipe", "vocab"), "dp"),
            P(),
        ),
        check_vma=False,
    )
```
